128 devices in a mesh: dp: 16 (over x, z_hi, core), tensor: 8 (over y, z_lo).
Axes of the slice: x: 4, y: 4, z: 4 (z_hi: 2, z_lo: 2; z = z_hi * 2 + z_lo), core: 2. Of those that a mesh axis runs over, the one named last changes fastest.
Arguments:
- gate_pre: bfloat16 [16384, 14336], P('dp', 'tensor'), may hold values from -6 to 6
- up_pre: bfloat16 [16384, 14336], P('dp', 'tensor'), may hold values from -6 to 6
- out_grad: bfloat16 [16384, 4096], P(('dp', 'tensor')), may hold values from -6 to 6
- w_blocks: bfloat16 [8, 16, 26, 128, 128], P('tensor', 'dp'), may hold values from -0.0625 to 0.0625
- block_ids: int32 [8, 16, 26], P('tensor', 'dp'), may hold values from 0 to 448, as said below
Outputs:
- mixed: bfloat16 [16384, 4096], P(('dp', 'tensor'))
- gate_grad: bfloat16 [16384, 14336], P('dp', 'tensor')
- up_grad: bfloat16 [16384, 14336], P('dp', 'tensor')
- block_grads: float32 [8, 16, 26, 128, 128], P('tensor', 'dp')
The draws below stay inside these ranges and needn't reach their ends.
Inputs may be any that keep to these rules, and one draw needn't show every extreme that they name: block_ids[t, o, s] is r * 32 + c for a nonzero block (r, c) of slice t's 14 x 32 block grid, or 448 for an empty slot; each nonzero block of a slice is listed exactly once among its owners; each block row holds exactly 16 nonzero blocks and each block column exactly 7; in every slice one owner fills all 26 slots.
All inputs are finite; a program needn't handle non-finite values.
Results may differ from the reference program's by a relative error of at most 0.017.
Values may be sent and summed in bfloat16 or wider, within the bound.
A program may use at most 192 MiB of HBM per device.

```python
import math
import jax
import jax.numpy as jnp
from jax import lax

D = 4096
FF = 14336
BLK = 128
TOK_DEV = 128
NFB = 14
NDB = 32
NLOC = 448
NB = 224
MAXB = 26
TOKENS = 16384
N_DP = 16
N_TENSOR = 8


def draw_block_ids(key, part):
    key = jax.random.fold_in(key, 7)

    def one_slice(slice_key):
        pair_key, column_key, order_key, owner_key = jax.random.split(slice_key, 4)
        pair_count = NDB // 2
        halves = NFB // 2
        shuffles = jax.vmap(lambda pair_seed: jax.random.permutation(pair_seed, NFB))(jax.random.split(pair_key, pair_count))
        places = jnp.argsort(shuffles, axis=1)
        upper_half = (places < halves).astype(jnp.int32)
        columns = jnp.stack([upper_half, 1 - upper_half], axis=1).reshape(NDB, NFB)
        mixing = jax.random.permutation(column_key, NDB)
        layout = columns[mixing].T
        flat_mask = layout.reshape(-1)
        scores = (1 - flat_mask) * NLOC + jax.random.permutation(order_key, NLOC).astype(jnp.int32)
        block_order = jnp.argsort(scores)[:NB].astype(jnp.int32)
        heavy_owner = jax.random.randint(owner_key, (), 0, N_DP).astype(jnp.int32)
        counter = jnp.arange(NB, dtype=jnp.int32)
        later_index = jnp.maximum(counter - MAXB, 0)
        other_owner = later_index % (N_DP - 1)
        other_owner = other_owner + (other_owner >= heavy_owner).astype(jnp.int32)
        owner_index = jnp.where(counter < MAXB, heavy_owner, other_owner)
        slot_index = jnp.where(counter < MAXB, counter, later_index // (N_DP - 1))
        return jnp.full((N_DP, MAXB), NLOC, jnp.int32).at[owner_index, slot_index].set(block_order)
    return jax.vmap(one_slice)(jax.random.split(key, N_TENSOR))


def shard_levels(stream_key, dims, pieces, smallest, largest):
    gain = 1.0
    for dim, shards_of in pieces:
        steps = jax.random.uniform(jax.random.fold_in(jax.random.fold_in(stream_key, 6), dim), (shards_of,), jnp.float32, smallest / len(pieces), largest / len(pieces))
        gain = gain * jnp.repeat(jnp.exp(steps), dims[dim] // shards_of).reshape((-1,) + (1,) * (len(dims) - 1 - dim))
    return gain


def normal_values(own_key, dims, width, most, cuts=(), kind=jnp.bfloat16):
    values = jax.random.normal(own_key, dims, jnp.float32) * width
    if len(cuts) > 0:
        values = shard_levels(own_key, dims, cuts, -0.22, 0.18) * values
    return jnp.clip(values, min=-most, max=most).astype(kind)


def setup_inputs(seed: int = 0) -> dict:
    key_list = jax.random.split(jax.random.key(seed), 6)
    gate_pre = normal_values(key_list[0], (TOKENS, FF), 1.0, 6.0, ((0, 16), (1, 8)))
    up_pre = normal_values(key_list[1], (TOKENS, FF), 1.0, 6.0, ((0, 16), (1, 8)))
    out_grad = normal_values(key_list[2], (TOKENS, D), 1.0, 6.0, ((0, 128),))
    w_blocks = normal_values(key_list[3], (N_TENSOR, N_DP, MAXB, BLK, BLK), (FF // 2) ** -0.5, 0.0625, ((0, 8), (1, 16)))
    block_ids = draw_block_ids(jax.random.fold_in(key_list[5], 71), 0)
    return {"gate_pre": gate_pre, "up_pre": up_pre, "out_grad": out_grad, "w_blocks": w_blocks, "block_ids": block_ids}


def block_orders(block_list, row_blocks, column_blocks):
    block_total = row_blocks * column_blocks
    slot_count = block_list.shape[0]
    matches = (block_list[None, :] == jnp.arange(block_total, dtype=jnp.int32)[:, None]).astype(jnp.int32)
    present = lax.optimization_barrier(jnp.sum(matches, axis=1, dtype=jnp.int32)).reshape(row_blocks, column_blocks)
    slot_index = lax.optimization_barrier(jnp.sum(matches * jnp.arange(slot_count, dtype=jnp.int32)[None, :], axis=1, dtype=jnp.int32)).reshape(row_blocks, column_blocks)
    rank_column = jnp.cumsum(present, axis=0, dtype=jnp.int32) - 1
    rank_row = jnp.cumsum(present, axis=1, dtype=jnp.int32) - 1
    column_pick = (present[:, :, None] == 1) & (rank_column[:, :, None] == jnp.arange(row_blocks // 2, dtype=jnp.int32)[None, None, :])
    column_rows = lax.optimization_barrier(jnp.sum(column_pick.astype(jnp.int32) * jnp.arange(row_blocks, dtype=jnp.int32)[:, None, None], axis=0, dtype=jnp.int32))
    row_pick = (present[:, :, None] == 1) & (rank_row[:, :, None] == jnp.arange(column_blocks // 2, dtype=jnp.int32)[None, None, :])
    row_columns = lax.optimization_barrier(jnp.sum(row_pick.astype(jnp.int32) * jnp.arange(column_blocks, dtype=jnp.int32)[None, :, None], axis=1, dtype=jnp.int32))
    column_slots = slot_index[column_rows, jnp.arange(column_blocks, dtype=jnp.int32)[:, None]]
    row_slots = slot_index[jnp.arange(row_blocks, dtype=jnp.int32)[:, None], row_columns]
    return (column_rows, row_columns, rank_column, column_slots, row_slots)

def pick_blocks(source, block_list, rank_column, row_blocks, column_blocks):
    is_used = block_list < row_blocks * column_blocks
    row_index = jnp.where(is_used, block_list // column_blocks, 0).astype(jnp.int32)
    column_index = jnp.where(is_used, block_list % column_blocks, 0).astype(jnp.int32)
    rank_index = jnp.maximum(rank_column[row_index, column_index], 0).astype(jnp.int32)
    return source[column_index, rank_index] * is_used.astype(source.dtype)[:, None, None]

def gated(gate_rows, up_rows):
    gate_value = gate_rows.astype(jnp.float32)
    return (jax.nn.silu(gate_value) * up_rows.astype(jnp.float32)).astype(jnp.bfloat16)

def input_grads(grad_hidden, gate_rows, up_rows):
    gate_value = gate_rows.astype(jnp.float32)
    up_value = up_rows.astype(jnp.float32)
    sigmoid_gate = jax.nn.sigmoid(gate_value)
    gate_grad = grad_hidden * up_value * sigmoid_gate * (1.0 + gate_value * (1.0 - sigmoid_gate))
    up_grad = grad_hidden * gate_value * sigmoid_gate
    return (gate_grad.astype(jnp.bfloat16), up_grad.astype(jnp.bfloat16))

def forward_rows(hidden_rows, by_column, column_rows):
    row_count = hidden_rows.shape[0]
    block_size = by_column.shape[-1]
    panels = hidden_rows.reshape(row_count, -1, block_size)[:, column_rows]
    result = jnp.einsum('tckr,ckrd->tcd', panels.astype(jnp.float32), by_column.astype(jnp.float32))
    return result.reshape(row_count, -1)

def backward_rows(grad_rows, by_row, row_columns):
    row_count = grad_rows.shape[0]
    block_size = by_row.shape[-1]
    panels = grad_rows.reshape(row_count, -1, block_size)[:, row_columns]
    result = jnp.einsum('trjd,rjkd->trk', panels.astype(jnp.float32), by_row.astype(jnp.float32))
    return result.reshape(row_count, -1)

def weight_rows(hidden_rows, grad_rows, column_rows):
    row_count = hidden_rows.shape[0]
    block_size = column_rows.shape[0] and grad_rows.shape[1] // column_rows.shape[0]
    panels = hidden_rows.reshape(row_count, -1, block_size)[:, column_rows]
    grad_panels = grad_rows.reshape(row_count, -1, block_size)
    return jnp.einsum('tckr,tcd->ckrd', panels.astype(jnp.float32), grad_panels.astype(jnp.float32))

def reference(gate_pre, up_pre, out_grad, w_blocks, block_ids):
    block_size = BLK
    slice_width = FF // N_TENSOR
    group_rows = TOK_DEV * N_TENSOR
    grad_scale = 1.0 / math.sqrt(TOKENS)
    mixed_sum = jnp.zeros((TOKENS, D), jnp.float32)
    gate_parts = []
    up_parts = []
    grad_parts = []
    grad_groups = out_grad.reshape(N_DP, group_rows, D)
    for tensor_index in range(N_TENSOR):
        block_list = block_ids[tensor_index].reshape(-1)
        weights = w_blocks[tensor_index].reshape(-1, block_size, block_size)
        column_rows, row_columns, rank_column, column_slots, row_slots = block_orders(block_list, NFB, NDB)
        by_column = weights[column_slots]
        by_row = weights[row_slots]
        lower = tensor_index * slice_width
        gate_part = gate_pre[:, lower:lower + slice_width].reshape(N_DP, group_rows, slice_width)
        up_part = up_pre[:, lower:lower + slice_width].reshape(N_DP, group_rows, slice_width)

        def group_step(summed, inputs):
            gate_rows, up_rows, grad_rows = inputs
            hidden_rows = gated(gate_rows, up_rows)
            part_out = lax.optimization_barrier(forward_rows(hidden_rows, by_column, column_rows).astype(jnp.bfloat16)).astype(jnp.float32)
            grad_hidden = backward_rows(grad_rows, by_row, row_columns)
            gate_grad, up_grad = input_grads(grad_hidden, gate_rows, up_rows)
            term = weight_rows(hidden_rows, grad_rows, column_rows) * grad_scale
            term = lax.optimization_barrier(term.astype(jnp.bfloat16)).astype(jnp.float32)
            return (summed + term, (part_out, gate_grad, up_grad))
        initial = jnp.zeros((NDB, NFB // 2, block_size, block_size), jnp.float32)
        summed, (parts, gate_grad, up_grad) = lax.scan(group_step, initial, (gate_part, up_part, grad_groups))
        mixed_sum = mixed_sum + parts.reshape(TOKENS, D)
        gate_parts.append(gate_grad.reshape(TOKENS, slice_width))
        up_parts.append(up_grad.reshape(TOKENS, slice_width))
        picked = pick_blocks(summed, block_list, rank_column, NFB, NDB)
        grad_parts.append(picked.reshape(N_DP, MAXB, block_size, block_size))
    return (mixed_sum.astype(jnp.bfloat16), jnp.concatenate(gate_parts, axis=1), jnp.concatenate(up_parts, axis=1), jnp.stack(grad_parts, axis=0))
```

```python
import functools
import math

import jax
import jax.numpy as jnp
from jax import lax
from jax.experimental import pallas as pl
from jax.experimental.pallas import tpu as pltpu
from jax.sharding import PartitionSpec as P

MESH = pl.DeviceIdType.MESH
BF = jnp.bfloat16
F32 = jnp.float32
ANY = pl.BlockSpec(memory_space=pl.ANY)
VM = pl.BlockSpec(memory_space=pltpu.VMEM)
MIB = 1024 * 1024

N_DP = 16
N_T = 8
BLK = 128
TOK = 128
NFB = 14
NDB = 32
NLOC = NFB * NDB
MAXB = 26
D = NDB * BLK
HID = NFB * BLK
ROWS = TOK * N_T
PIECE = MAXB * BLK
META = 16
WROWS = PIECE + META
WHALF = 1680


def flip_core(i):
    return i + 1 - 2 * (i % 2)


def flip_far(i):
    return i + 2 - 4 * ((i // 2) % 2)


def greet(devices):
    barrier = pltpu.get_barrier_semaphore()
    for device in devices:
        pl.semaphore_signal(barrier, inc=1, device_id=device, device_id_type=MESH)
    pl.semaphore_wait(barrier, len(devices))


class Sends:
    def __init__(self, send, recv):
        self.send, self.recv, self.started = send, recv, []

    def start(self, i, src, dst, device):
        copy = pltpu.make_async_remote_copy(
            src, dst, self.send.at[i], self.recv.at[i], device_id=device, device_id_type=MESH
        )
        copy.start()
        self.started.append(copy)

    def arrived(self, i, dst, device):
        pltpu.make_async_remote_copy(
            dst, dst, self.send.at[i], self.recv.at[i], device_id=device, device_id_type=MESH
        ).wait_recv()

    def finish(self):
        for copy in self.started:
            copy.wait_send()


def gather_kernel(
    g_ref, w_ref, gate_ref, up_ref, g_all, w_all, h_out, ht_out,
    gate_v, up_v, h_v, ht_v, g_send, g_recv, w_send, w_recv, loc,
):
    dp, t = lax.axis_index("dp"), lax.axis_index("tensor")
    z, yp, ym, y2 = flip_core(t), (t + 2) % N_T, (t + 6) % N_T, (t + 4) % N_T
    h, xp, xm, x2 = flip_far(dp), (dp + 4) % N_DP, (dp + 12) % N_DP, (dp + 8) % N_DP
    c = flip_core(dp)
    Z, YP, YM = (dp, z), (dp, yp), (dp, ym)
    H, XP, XM, C = (h, t), (xp, t), (xm, t), (c, t)

    local = [
        pltpu.make_async_copy(gate_ref, gate_v, loc.at[0]),
        pltpu.make_async_copy(up_ref, up_v, loc.at[1]),
        pltpu.make_async_copy(g_ref, g_all.at[t], loc.at[2]),
        pltpu.make_async_copy(w_ref, w_all.at[dp], loc.at[3]),
    ]
    for copy in local:
        copy.start()
    greet((Z, YP, YM, H, XP, XM, C))

    g, w = Sends(g_send, g_recv), Sends(w_send, w_recv)
    lo, hi = pl.ds(0, TOK // 2), pl.ds(TOK // 2, TOK // 2)
    wlo, whi = pl.ds(0, WHALF), pl.ds(WHALF, WROWS - WHALF)

    g.start(0, g_ref, g_all.at[t], Z)
    w.start(0, w_ref, w_all.at[dp], H)
    g.start(1, g_ref, g_all.at[t], YP)
    g.start(2, g_ref, g_all.at[t], YM)
    w.start(1, w_ref, w_all.at[dp], XP)
    w.start(2, w_ref, w_all.at[dp], XM)
    w.start(9, w_ref, w_all.at[dp], C)

    local[0].wait()
    local[1].wait()

    @pl.loop(0, ROWS // TOK)
    def _(i):
        rows = pl.ds(pl.multiple_of(i * TOK, TOK), TOK)
        for b in range(NFB):
            cols = pl.ds(b * BLK, BLK)
            gate = gate_v[rows, cols].astype(F32)
            hid = (gate * jax.nn.sigmoid(gate) * up_v[rows, cols].astype(F32)).astype(BF)
            h_v[rows, cols] = hid
            ht_v[cols, rows] = hid.T

    outs = [
        pltpu.make_async_copy(h_v, h_out, loc.at[4]),
        pltpu.make_async_copy(ht_v, ht_out, loc.at[5]),
    ]
    for copy in outs:
        copy.start()

    w.arrived(1, w_all.at[xm], XM)
    w.start(5, w_all.at[xm, wlo], w_all.at[xm, wlo], XP)
    w.start(11, w_all.at[xm], w_all.at[xm], C)
    w.arrived(2, w_all.at[xp], XP)
    w.start(6, w_all.at[xp, whi], w_all.at[xp, whi], XM)
    w.start(12, w_all.at[xp], w_all.at[xp], C)

    g.arrived(0, g_all.at[z], Z)
    g.start(3, g_all.at[z], g_all.at[z], YP)
    g.start(4, g_all.at[z], g_all.at[z], YM)
    g.arrived(1, g_all.at[ym], YM)
    g.start(5, g_all.at[ym, lo], g_all.at[ym, lo], YP)
    g.arrived(2, g_all.at[yp], YP)
    g.start(6, g_all.at[yp, hi], g_all.at[yp, hi], YM)

    w.arrived(0, w_all.at[h], H)
    w.start(3, w_all.at[h], w_all.at[h], XP)
    w.start(4, w_all.at[h], w_all.at[h], XM)
    w.start(10, w_all.at[h], w_all.at[h], C)

    w.arrived(5, w_all.at[x2, wlo], XM)
    w.start(15, w_all.at[x2, wlo], w_all.at[x2, wlo], C)
    w.arrived(6, w_all.at[x2, whi], XP)
    w.start(16, w_all.at[x2, whi], w_all.at[x2, whi], C)

    zm, zp, z2 = flip_core(ym), flip_core(yp), flip_core(y2)
    g.arrived(3, g_all.at[zm], YM)
    g.start(7, g_all.at[zm, lo], g_all.at[zm, lo], YP)
    g.arrived(4, g_all.at[zp], YP)
    g.start(8, g_all.at[zp, hi], g_all.at[zp, hi], YM)

    hm, hp, h2 = flip_far(xm), flip_far(xp), flip_far(x2)
    w.arrived(3, w_all.at[hm], XM)
    w.start(7, w_all.at[hm, wlo], w_all.at[hm, wlo], XP)
    w.start(13, w_all.at[hm], w_all.at[hm], C)
    w.arrived(4, w_all.at[hp], XP)
    w.start(8, w_all.at[hp, whi], w_all.at[hp, whi], XM)
    w.start(14, w_all.at[hp], w_all.at[hp], C)
    w.arrived(7, w_all.at[h2, wlo], XM)
    w.start(17, w_all.at[h2, wlo], w_all.at[h2, wlo], C)
    w.arrived(8, w_all.at[h2, whi], XP)
    w.start(18, w_all.at[h2, whi], w_all.at[h2, whi], C)

    g.arrived(5, g_all.at[y2, lo], YM)
    g.arrived(6, g_all.at[y2, hi], YP)
    g.arrived(7, g_all.at[z2, lo], YM)
    g.arrived(8, g_all.at[z2, hi], YP)
    for i, source in ((9, dp), (10, h), (11, xm), (12, xp), (13, hm), (14, hp)):
        w.arrived(i, w_all.at[flip_core(source)], C)
    for i, source, part in ((15, x2, wlo), (16, x2, whi), (17, h2, wlo), (18, h2, whi)):
        w.arrived(i, w_all.at[flip_core(source), part], C)
    g.finish()
    w.finish()
    for copy in (local[2], local[3], outs[0], outs[1]):
        copy.wait()


def compute_kernel(
    scale, gate_ref, up_ref, h_ref, ht_ref, g_ref, w_ref, p_out, q_out, gg_out, ug_out,
    wd, h_v, ht_v, g_v, blocks, gate_v, up_v, meta_v, ids_v, ids_s, p_v, zero_v,
    loc, wsem, psem, qsem, osem,
):
    loads = [
        pltpu.make_async_copy(w_ref.at[:, pl.ds(PIECE, META)], meta_v, loc.at[0]),
        pltpu.make_async_copy(ht_ref, ht_v, loc.at[1]),
        pltpu.make_async_copy(g_ref, g_v, loc.at[2]),
        pltpu.make_async_copy(h_ref, h_v, loc.at[3]),
        pltpu.make_async_copy(gate_ref, gate_v, loc.at[4]),
        pltpu.make_async_copy(up_ref, up_v, loc.at[5]),
    ]
    for copy in loads:
        copy.start()

    @pl.loop(0, HID // 16)
    def _(i):
        wd[pl.ds(pl.multiple_of(i * 16, 16), 16), :] = jnp.zeros((16, D), BF)

    zero_v[...] = jnp.zeros((BLK, BLK), BF)
    loads[0].wait()
    for o in range(N_DP):
        both = meta_v[o].astype(F32)
        ids_v[o : o + 1, :] = (both[0:1, :] * NDB + both[1:2, :]).astype(jnp.int32)
    to_scalar = pltpu.make_async_copy(ids_v, ids_s, loc.at[6])
    to_scalar.start()
    to_scalar.wait()

    def place(o, s):
        b = ids_s[o, s]
        row = pl.multiple_of((b // NDB) * BLK, BLK)
        col = pl.multiple_of((b % NDB) * BLK, BLK)
        return b, row, col

    def w_copy(o, s):
        b, row, col = place(o, s)
        src = w_ref.at[o, pl.ds(pl.multiple_of(s * BLK, BLK), BLK), :]
        return b, pltpu.make_async_copy(src, wd.at[pl.ds(row, BLK), pl.ds(col, BLK)], wsem)

    @pl.loop(0, N_DP)
    def _(o):
        @pl.loop(0, MAXB)
        def _(s):
            b, copy = w_copy(o, s)

            @pl.when(b < NLOC)
            def _():
                copy.start()

    loads[1].wait()
    loads[2].wait()

    TN = 256

    @pl.loop(0, D // TN)
    def _(j):
        for i in range(2):
            rows = HID // 2
            cols = pl.ds(pl.multiple_of(j * TN, TN), TN)
            res = jnp.dot(ht_v[i * rows : (i + 1) * rows, :], g_v[:, cols], preferred_element_type=F32)
            res = (res * scale).astype(BF)
            for cb in range(TN // BLK):
                for rb in range(NFB // 2):
                    blocks[(j * (TN // BLK) + cb) * NFB + i * (NFB // 2) + rb] = res[
                        rb * BLK : (rb + 1) * BLK, cb * BLK : (cb + 1) * BLK
                    ]

    def q_copy(o, s, src):
        dst = q_out.at[o, pl.ds(pl.multiple_of(s * BLK, BLK), BLK), :]
        return pltpu.make_async_copy(src, dst, qsem)

    @pl.loop(0, N_DP)
    def _(o):
        @pl.loop(0, MAXB)
        def _(s):
            b = ids_s[o, s]

            @pl.when(b < NLOC)
            def _():
                q_copy(o, s, blocks.at[(b % NDB) * NFB + b // NDB]).start()

            @pl.when(b >= NLOC)
            def _():
                q_copy(o, s, zero_v).start()

    @pl.loop(0, N_DP)
    def _(o):
        @pl.loop(0, MAXB)
        def _(s):
            b, copy = w_copy(o, s)

            @pl.when(b < NLOC)
            def _():
                copy.wait()

    loads[3].wait()
    PN = 512

    def p_copy(j, slot):
        cols = pl.ds(pl.multiple_of(j * PN, PN), PN)
        return pltpu.make_async_copy(p_v.at[slot], p_out.at[:, cols], psem.at[slot])

    @pl.loop(0, D // PN)
    def _(j):
        slot = j % 2

        @pl.when(j >= 2)
        def _():
            p_copy(j - 2, slot).wait()

        for i in range(2):
            rows = slice(i * ROWS // 2, (i + 1) * ROWS // 2)
            cols = pl.ds(pl.multiple_of(j * PN, PN), PN)
            p_v[slot, rows, :] = jnp.dot(h_v[rows, :], wd[:, cols], preferred_element_type=F32).astype(BF)
        p_copy(j, slot).start()

    p_copy(D // PN - 2, 0).wait()
    p_copy(D // PN - 1, 1).wait()

    loads[4].wait()
    loads[5].wait()
    BN = 256

    def o_copies(j):
        cols = pl.ds(pl.multiple_of(j * BN, BN), BN)
        return (
            pltpu.make_async_copy(gate_v.at[:, cols], gg_out.at[:, cols], osem.at[0, j]),
            pltpu.make_async_copy(up_v.at[:, cols], ug_out.at[:, cols], osem.at[1, j]),
        )

    @pl.loop(0, HID // BN)
    def _(j):
        cols = pl.ds(pl.multiple_of(j * BN, BN), BN)
        for i in range(2):
            rows = slice(i * ROWS // 2, (i + 1) * ROWS // 2)
            gh = lax.dot_general(
                g_v[rows, :], wd[cols, :], (((1,), (1,)), ((), ())), preferred_element_type=F32
            )
            gate = gate_v[rows, cols].astype(F32)
            up = up_v[rows, cols].astype(F32)
            sig = jax.nn.sigmoid(gate)
            gate_v[rows, cols] = (gh * up * sig * (1.0 + gate * (1.0 - sig))).astype(BF)
            up_v[rows, cols] = (gh * gate * sig).astype(BF)
        for copy in o_copies(j):
            copy.start()

    @pl.loop(0, HID // BN)
    def _(j):
        for copy in o_copies(j):
            copy.wait()

    @pl.loop(0, N_DP)
    def _(o):
        @pl.loop(0, MAXB)
        def _(s):
            q_copy(o, s, zero_v).wait()


def add_rows(dst, sources, rows, step):
    @pl.loop(0, rows // step)
    def _(i):
        part = pl.ds(pl.multiple_of(i * step, step), step)
        total = sources[0][part, :].astype(F32)
        for source in sources[1:]:
            total = total + source[part, :].astype(F32)
        dst[part, :] = total.astype(dst.dtype)


def scatter_kernel(
    p_ref, q_ref, mixed_ref, bg_ref,
    pa, pb, po, prel, pm, pp, pz, qv, qc, qrel, qm, qp, qh,
    m_send, m_recv, q_send, q_recv, ploc, qloc,
):
    dp, t = lax.axis_index("dp"), lax.axis_index("tensor")
    z, yp, ym, y2 = flip_core(t), (t + 2) % N_T, (t + 6) % N_T, (t + 4) % N_T
    h, xp, xm = flip_far(dp), (dp + 4) % N_DP, (dp + 12) % N_DP
    c = flip_core(dp)
    Z, YP, YM = (dp, z), (dp, yp), (dp, ym)
    H, XP, XM, C = (h, t), (xp, t), (xm, t), (c, t)
    x, core = dp // 4, dp % 2
    xpi, xmi, x2i = (x + 1) % 4, (x + 3) % 4, (x + 2) % 4
    zh, zl = (dp // 2) % 2, t % 2
    ybase, ypb, ymb, y2b = t - zl, yp - zl, ym - zl, y2 - zl

    ploads = [
        pltpu.make_async_copy(p_ref.at[ypb], pa, ploc.at[0]),
        pltpu.make_async_copy(p_ref.at[ymb + 1], pb, ploc.at[1]),
        pltpu.make_async_copy(p_ref.at[ybase], po.at[0], ploc.at[2]),
        pltpu.make_async_copy(p_ref.at[ybase + 1], po.at[1], ploc.at[3]),
    ]
    order = [(x2i, 0), (x2i, 1), (xpi, 1), (xmi, 0), (xpi, 0), (xmi, 1), (x, 0), (x, 1)]
    qloads = [
        pltpu.make_async_copy(q_ref.at[(xi * 4 + p * 2) + core], qv.at[k], qloc.at[k])
        for k, (xi, p) in enumerate(order)
    ]
    for copy in qloads + ploads:
        copy.start()
    greet((Z, YP, YM, H, XP, XM, C))

    m, q = Sends(m_send, m_recv), Sends(q_send, q_recv)
    for k, (xi, p) in enumerate(order[:2]):
        q.start(7 + k, q_ref.at[(xi * 4 + p * 2) + 1 - core], qc.at[k], C)
    m.start(0, p_ref.at[y2b], prel.at[0], YP)
    m.start(1, p_ref.at[y2b + 1], prel.at[1], YM)
    m.start(2, p_ref.at[ypb + 1], pm.at[1], YP)
    m.start(3, p_ref.at[ymb], pp.at[0], YM)
    for k, (xi, p) in enumerate(order):
        if k >= 2:
            q.start(7 + k, q_ref.at[(xi * 4 + p * 2) + 1 - core], qc.at[k], C)

    def add_sibling(k, extra=()):
        q.arrived(7 + k, qc.at[k], C)
        qloads[k].wait()
        add_rows(qv.at[k], [qv.at[k], qc.at[k], *extra], PIECE, 208)

    add_sibling(0)
    q.start(0, qv.at[0], qrel.at[0], XP)
    add_sibling(1)
    q.start(1, qv.at[1], qrel.at[1], XM)
    add_sibling(2)
    q.start(2, qv.at[2], qm.at[1], XP)
    add_sibling(3)
    q.start(3, qv.at[3], qp.at[0], XM)

    q.arrived(0, qrel.at[0], XM)
    add_sibling(4, [qrel.at[0]])
    q.start(4, qv.at[4], qm.at[0], XP)
    q.arrived(1, qrel.at[1], XP)
    add_sibling(5, [qrel.at[1]])
    q.start(5, qv.at[5], qp.at[1], XM)

    ploads[0].wait()
    m.arrived(0, prel.at[0], YM)
    add_rows(pa, [pa, prel.at[0]], TOK, 16)
    m.start(4, pa, pm.at[0], YP)
    ploads[1].wait()
    m.arrived(1, prel.at[1], YP)
    add_rows(pb, [pb, prel.at[1]], TOK, 16)
    m.start(5, pb, pp.at[1], YM)

    for k in (6, 7):
        q.arrived(7 + k, qc.at[k], C)
        qloads[k].wait()
    q.arrived(2, qm.at[1], XM)
    q.arrived(3, qp.at[0], XP)
    q.arrived(4, qm.at[0], XM)
    q.arrived(5, qp.at[1], XP)
    add_rows(qv.at[7 - zh], [qv.at[7 - zh], qc.at[7 - zh], qm.at[1 - zh], qp.at[1 - zh]], PIECE, 208)
    q.start(6, qv.at[7 - zh], qh, H)

    ploads[2].wait()
    ploads[3].wait()
    m.arrived(2, pm.at[1], YM)
    m.arrived(3, pp.at[0], YP)
    m.arrived(4, pm.at[0], YM)
    m.arrived(5, pp.at[1], YP)
    add_rows(po.at[1 - zl], [po.at[1 - zl], pm.at[1 - zl], pp.at[1 - zl]], TOK, 16)
    m.start(6, po.at[1 - zl], pz, Z)

    q.arrived(6, qh, H)
    add_rows(bg_ref, [qv.at[6 + zh], qc.at[6 + zh], qm.at[zh], qp.at[zh], qh], PIECE, 208)
    m.arrived(6, pz, Z)
    add_rows(mixed_ref, [po.at[zl], pm.at[zl], pp.at[zl], pz], TOK, 16)
    m.finish()
    q.finish()


def local(gate_pre, up_pre, out_grad, w_blocks, block_ids):
    scale = 1.0 / math.sqrt(ROWS * N_DP)
    ids = block_ids[0, 0]
    meta = jnp.zeros((META, BLK), BF)
    meta = meta.at[0, :MAXB].set((ids // NDB).astype(BF)).at[1, :MAXB].set((ids % NDB).astype(BF))
    packed = jnp.concatenate([w_blocks.reshape(PIECE, BLK), meta], axis=0)

    sem = pltpu.SemaphoreType.DMA
    g_all, w_all, hid, hid_t = pl.pallas_call(
        gather_kernel,
        out_shape=(
            jax.ShapeDtypeStruct((N_T, TOK, D), BF),
            jax.ShapeDtypeStruct((N_DP, WROWS, BLK), BF),
            jax.ShapeDtypeStruct((ROWS, HID), BF),
            jax.ShapeDtypeStruct((HID, ROWS), BF),
        ),
        in_specs=[ANY] * 4,
        out_specs=[ANY] * 4,
        scratch_shapes=[
            pltpu.VMEM((ROWS, HID), BF),
            pltpu.VMEM((ROWS, HID), BF),
            pltpu.VMEM((ROWS, HID), BF),
            pltpu.VMEM((HID, ROWS), BF),
            sem((9,)), sem((9,)), sem((19,)), sem((19,)), sem((6,)),
        ],
        compiler_params=pltpu.CompilerParams(
            collective_id=0, has_side_effects=True, vmem_limit_bytes=40 * MIB
        ),
        name="gather",
    )(out_grad, packed, gate_pre, up_pre)

    parts, packed_grads, gate_grad, up_grad = pl.pallas_call(
        functools.partial(compute_kernel, scale),
        out_shape=(
            jax.ShapeDtypeStruct((ROWS, D), BF),
            jax.ShapeDtypeStruct((N_DP, PIECE, BLK), BF),
            jax.ShapeDtypeStruct((ROWS, HID), BF),
            jax.ShapeDtypeStruct((ROWS, HID), BF),
        ),
        in_specs=[ANY] * 6,
        out_specs=[ANY] * 4,
        scratch_shapes=[
            pltpu.VMEM((HID, D), BF),
            pltpu.VMEM((ROWS, HID), BF),
            pltpu.VMEM((HID, ROWS), BF),
            pltpu.VMEM((ROWS, D), BF),
            pltpu.VMEM((NLOC, BLK, BLK), BF),
            pltpu.VMEM((ROWS, HID), BF),
            pltpu.VMEM((ROWS, HID), BF),
            pltpu.VMEM((N_DP, META, BLK), BF),
            pltpu.VMEM((N_DP, BLK), jnp.int32),
            pltpu.SMEM((N_DP, BLK), jnp.int32),
            pltpu.VMEM((2, ROWS, 512), BF),
            pltpu.VMEM((BLK, BLK), BF),
            sem((7,)), sem, sem((2,)), sem, sem((2, 7)),
        ],
        compiler_params=pltpu.CompilerParams(vmem_limit_bytes=60 * MIB),
        name="compute",
    )(gate_pre, up_pre, hid, hid_t, g_all.reshape(ROWS, D), w_all)

    mixed, grads = pl.pallas_call(
        scatter_kernel,
        out_shape=(
            jax.ShapeDtypeStruct((TOK, D), BF),
            jax.ShapeDtypeStruct((PIECE, BLK), F32),
        ),
        in_specs=[ANY] * 2,
        out_specs=[VM] * 2,
        scratch_shapes=[
            pltpu.VMEM((TOK, D), BF),
            pltpu.VMEM((TOK, D), BF),
            pltpu.VMEM((2, TOK, D), BF),
            pltpu.VMEM((2, TOK, D), BF),
            pltpu.VMEM((2, TOK, D), BF),
            pltpu.VMEM((2, TOK, D), BF),
            pltpu.VMEM((TOK, D), BF),
            pltpu.VMEM((8, PIECE, BLK), BF),
            pltpu.VMEM((8, PIECE, BLK), BF),
            pltpu.VMEM((2, PIECE, BLK), BF),
            pltpu.VMEM((2, PIECE, BLK), BF),
            pltpu.VMEM((2, PIECE, BLK), BF),
            pltpu.VMEM((PIECE, BLK), BF),
            sem((7,)), sem((7,)), sem((15,)), sem((15,)), sem((4,)), sem((8,)),
        ],
        compiler_params=pltpu.CompilerParams(
            collective_id=1, has_side_effects=True, vmem_limit_bytes=56 * MIB
        ),
        name="scatter",
    )(parts.reshape(N_T, TOK, D), packed_grads)
    return mixed, gate_grad, up_grad, grads.reshape(1, 1, MAXB, BLK, BLK)


def solution(mesh):
    placed = (
        P("dp", "tensor"),
        P("dp", "tensor"),
        P(("dp", "tensor"), None),
        P("tensor", "dp", None, None, None),
        P("tensor", "dp", None),
    )
    return jax.shard_map(
        local,
        mesh=mesh,
        in_specs=placed,
        out_specs=(
            P(("dp", "tensor"), None),
            P("dp", "tensor"),
            P("dp", "tensor"),
            P("tensor", "dp", None, None, None),
        ),
        check_vma=False,
    )
```

```python
import functools
import math

import jax
import jax.numpy as jnp
from jax import lax
from jax.experimental import pallas as pl
from jax.experimental.pallas import tpu as pltpu
from jax.sharding import PartitionSpec as P

MESH = pl.DeviceIdType.MESH
BF = jnp.bfloat16
F32 = jnp.float32
ANY = pl.BlockSpec(memory_space=pl.ANY)
VM = pl.BlockSpec(memory_space=pltpu.VMEM)
MIB = 1024 * 1024

N_DP = 16
N_T = 8
BLK = 128
TOK = 128
NFB = 14
NDB = 32
NLOC = NFB * NDB
MAXB = 26
D = NDB * BLK
HID = NFB * BLK
ROWS = TOK * N_T
PIECE = MAXB * BLK
META = 16
WROWS = PIECE + META
WHALF = 1680


def flip_core(i):
    return i + 1 - 2 * (i % 2)


def flip_far(i):
    return i + 2 - 4 * ((i // 2) % 2)


def greet(devices):
    barrier = pltpu.get_barrier_semaphore()
    for device in devices:
        pl.semaphore_signal(barrier, inc=1, device_id=device, device_id_type=MESH)
    pl.semaphore_wait(barrier, len(devices))


class Sends:
    def __init__(self, send, recv):
        self.send, self.recv, self.started = send, recv, []

    def start(self, i, src, dst, device):
        copy = pltpu.make_async_remote_copy(
            src, dst, self.send.at[i], self.recv.at[i], device_id=device, device_id_type=MESH
        )
        copy.start()
        self.started.append(copy)

    def arrived(self, i, dst, device):
        pltpu.make_async_remote_copy(
            dst, dst, self.send.at[i], self.recv.at[i], device_id=device, device_id_type=MESH
        ).wait_recv()

    def finish(self):
        for copy in self.started:
            copy.wait_send()


def gather_kernel(
    g_ref, w_ref, gate_ref, up_ref, g_all, w_all, h_out, ht_out,
    gate_v, up_v, h_v, ht_v, g_send, g_recv, w_send, w_recv, loc,
):
    dp, t = lax.axis_index("dp"), lax.axis_index("tensor")
    z, yp, ym, y2 = flip_core(t), (t + 2) % N_T, (t + 6) % N_T, (t + 4) % N_T
    h, xp, xm, x2 = flip_far(dp), (dp + 4) % N_DP, (dp + 12) % N_DP, (dp + 8) % N_DP
    c = flip_core(dp)
    Z, YP, YM = (dp, z), (dp, yp), (dp, ym)
    H, XP, XM, C = (h, t), (xp, t), (xm, t), (c, t)

    local = [
        pltpu.make_async_copy(gate_ref, gate_v, loc.at[0]),
        pltpu.make_async_copy(up_ref, up_v, loc.at[1]),
        pltpu.make_async_copy(g_ref, g_all.at[t], loc.at[2]),
        pltpu.make_async_copy(w_ref, w_all.at[dp], loc.at[3]),
    ]
    for copy in local:
        copy.start()
    greet((Z, YP, YM, H, XP, XM, C))

    g, w = Sends(g_send, g_recv), Sends(w_send, w_recv)
    lo, hi = pl.ds(0, TOK // 2), pl.ds(TOK // 2, TOK // 2)
    first, mid_lo, mid_hi, last = pl.ds(0, 16), pl.ds(16, 48), pl.ds(64, 48), pl.ds(112, 16)
    wlo, whi = pl.ds(0, WHALF), pl.ds(WHALF, WROWS - WHALF)

    g.start(0, g_ref, g_all.at[t], Z)
    w.start(0, w_ref, w_all.at[dp], H)
    g.start(1, g_ref, g_all.at[t], YP)
    g.start(2, g_ref, g_all.at[t], YM)
    w.start(1, w_ref, w_all.at[dp], XP)
    w.start(2, w_ref, w_all.at[dp], XM)
    w.start(9, w_ref, w_all.at[dp], C)

    local[0].wait()
    local[1].wait()

    @pl.loop(0, ROWS // TOK)
    def _(i):
        rows = pl.ds(pl.multiple_of(i * TOK, TOK), TOK)
        for b in range(NFB):
            cols = pl.ds(b * BLK, BLK)
            gate = gate_v[rows, cols].astype(F32)
            hid = (gate * jax.nn.sigmoid(gate) * up_v[rows, cols].astype(F32)).astype(BF)
            h_v[rows, cols] = hid
            ht_v[cols, rows] = hid.T

    outs = [
        pltpu.make_async_copy(h_v, h_out, loc.at[4]),
        pltpu.make_async_copy(ht_v, ht_out, loc.at[5]),
    ]
    for copy in outs:
        copy.start()

    w.arrived(1, w_all.at[xm], XM)
    w.start(5, w_all.at[xm, wlo], w_all.at[xm, wlo], XP)
    w.start(11, w_all.at[xm], w_all.at[xm], C)
    w.arrived(2, w_all.at[xp], XP)
    w.start(6, w_all.at[xp, whi], w_all.at[xp, whi], XM)
    w.start(12, w_all.at[xp], w_all.at[xp], C)

    g.arrived(1, g_all.at[ym], YM)
    g.start(5, g_all.at[ym, lo], g_all.at[ym, lo], YP)
    g.arrived(2, g_all.at[yp], YP)
    g.start(6, g_all.at[yp, hi], g_all.at[yp, hi], YM)
    g.arrived(0, g_all.at[z], Z)
    g.start(3, g_all.at[z], g_all.at[z], YP)
    g.start(4, g_all.at[z], g_all.at[z], YM)

    w.arrived(0, w_all.at[h], H)
    w.start(3, w_all.at[h], w_all.at[h], XP)
    w.start(4, w_all.at[h], w_all.at[h], XM)
    w.start(10, w_all.at[h], w_all.at[h], C)

    w.arrived(5, w_all.at[x2, wlo], XM)
    w.start(15, w_all.at[x2, wlo], w_all.at[x2, wlo], C)
    w.arrived(6, w_all.at[x2, whi], XP)
    w.start(16, w_all.at[x2, whi], w_all.at[x2, whi], C)

    zm, zp, z2 = flip_core(ym), flip_core(yp), flip_core(y2)
    g.arrived(5, g_all.at[y2, lo], YM)
    g.start(9, g_all.at[y2, mid_lo], g_all.at[y2, mid_lo], Z)
    g.arrived(6, g_all.at[y2, hi], YP)
    g.start(10, g_all.at[y2, mid_hi], g_all.at[y2, mid_hi], Z)
    g.arrived(3, g_all.at[zm], YM)
    g.start(7, g_all.at[zm, first], g_all.at[zm, first], YP)
    g.arrived(4, g_all.at[zp], YP)
    g.start(8, g_all.at[zp, last], g_all.at[zp, last], YM)

    hm, hp, h2 = flip_far(xm), flip_far(xp), flip_far(x2)
    w.arrived(3, w_all.at[hm], XM)
    w.start(7, w_all.at[hm, wlo], w_all.at[hm, wlo], XP)
    w.start(13, w_all.at[hm], w_all.at[hm], C)
    w.arrived(4, w_all.at[hp], XP)
    w.start(8, w_all.at[hp, whi], w_all.at[hp, whi], XM)
    w.start(14, w_all.at[hp], w_all.at[hp], C)
    w.arrived(7, w_all.at[h2, wlo], XM)
    w.start(17, w_all.at[h2, wlo], w_all.at[h2, wlo], C)
    w.arrived(8, w_all.at[h2, whi], XP)
    w.start(18, w_all.at[h2, whi], w_all.at[h2, whi], C)

    g.arrived(7, g_all.at[z2, first], YM)
    g.arrived(8, g_all.at[z2, last], YP)
    g.arrived(9, g_all.at[z2, mid_lo], Z)
    g.arrived(10, g_all.at[z2, mid_hi], Z)
    for i, source in ((9, dp), (10, h), (11, xm), (12, xp), (13, hm), (14, hp)):
        w.arrived(i, w_all.at[flip_core(source)], C)
    for i, source, part in ((15, x2, wlo), (16, x2, whi), (17, h2, wlo), (18, h2, whi)):
        w.arrived(i, w_all.at[flip_core(source), part], C)
    g.finish()
    w.finish()
    for copy in (local[2], local[3], outs[0], outs[1]):
        copy.wait()


def weight_kernel(
    scale, ht_ref, g_ref, w_ref, q_out, wd_out,
    wd, ht_v, g_v, blocks, meta_v, ids_v, ids_s, zero_v, loc, wsem, qsem,
):
    loads = [
        pltpu.make_async_copy(w_ref.at[:, pl.ds(PIECE, META)], meta_v, loc.at[0]),
        pltpu.make_async_copy(ht_ref, ht_v, loc.at[1]),
        pltpu.make_async_copy(g_ref, g_v, loc.at[2]),
    ]
    for copy in loads:
        copy.start()

    @pl.loop(0, HID // 16)
    def _(i):
        wd[pl.ds(pl.multiple_of(i * 16, 16), 16), :] = jnp.zeros((16, D), BF)

    zero_v[...] = jnp.zeros((BLK, BLK), BF)
    loads[0].wait()
    for o in range(N_DP):
        both = meta_v[o].astype(F32)
        ids_v[o : o + 1, :] = (both[0:1, :] * NDB + both[1:2, :]).astype(jnp.int32)
    to_scalar = pltpu.make_async_copy(ids_v, ids_s, loc.at[3])
    to_scalar.start()
    to_scalar.wait()

    def w_copy(o, s):
        b = ids_s[o, s]
        row = pl.multiple_of((b // NDB) * BLK, BLK)
        col = pl.multiple_of((b % NDB) * BLK, BLK)
        src = w_ref.at[o, pl.ds(pl.multiple_of(s * BLK, BLK), BLK), :]
        return b, pltpu.make_async_copy(src, wd.at[pl.ds(row, BLK), pl.ds(col, BLK)], wsem)

    @pl.loop(0, N_DP)
    def _(o):
        @pl.loop(0, MAXB)
        def _(s):
            b, copy = w_copy(o, s)

            @pl.when(b < NLOC)
            def _():
                copy.start()

    loads[1].wait()
    loads[2].wait()
    TN = 512

    @pl.loop(0, D // TN)
    def _(j):
        for i in range(2):
            rows = HID // 2
            cols = pl.ds(pl.multiple_of(j * TN, TN), TN)
            res = jnp.dot(ht_v[i * rows : (i + 1) * rows, :], g_v[:, cols], preferred_element_type=F32)
            res = (res * scale).astype(BF)
            for cb in range(TN // BLK):
                for rb in range(NFB // 2):
                    blocks[(j * (TN // BLK) + cb) * NFB + i * (NFB // 2) + rb] = res[
                        rb * BLK : (rb + 1) * BLK, cb * BLK : (cb + 1) * BLK
                    ]

    def q_copy(o, s, src):
        dst = q_out.at[o, pl.ds(pl.multiple_of(s * BLK, BLK), BLK), :]
        return pltpu.make_async_copy(src, dst, qsem)

    @pl.loop(0, N_DP)
    def _(o):
        @pl.loop(0, MAXB)
        def _(s):
            b, copy = w_copy(o, s)

            @pl.when(b < NLOC)
            def _():
                copy.wait()
                q_copy(o, s, blocks.at[(b % NDB) * NFB + b // NDB]).start()

            @pl.when(b >= NLOC)
            def _():
                q_copy(o, s, zero_v).start()

    dense = pltpu.make_async_copy(wd, wd_out, loc.at[4])
    dense.start()

    @pl.loop(0, N_DP)
    def _(o):
        @pl.loop(0, MAXB)
        def _(s):
            q_copy(o, s, zero_v).wait()

    dense.wait()


def add_rows(dst, sources, rows, step):
    @pl.loop(0, rows // step)
    def _(i):
        part = pl.ds(pl.multiple_of(i * step, step), step)
        total = sources[0][part, :].astype(F32)
        for source in sources[1:]:
            total = total + source[part, :].astype(F32)
        dst[part, :] = total.astype(dst.dtype)


NCH = 8
CW = D // NCH
NSP = 2
SR = PIECE // NSP
BN = 256
NBW = HID // BN
QSLOTS = 8


def scatter_kernel(
    gate_ref, up_ref, h_ref, wd_ref, g_ref, q_ref, mixed_ref, bg_ref, gg_out, ug_out,
    h_v, wd, g_v, gate_v, up_v, pv, prel, pm, pp, pz, qv, qc, qrel, qm, qp, qh,
    m_send, m_recv, q_send, q_recv, loc, wloc, qloc, bloc, oloc,
):
    dp, t = lax.axis_index("dp"), lax.axis_index("tensor")
    z, yp, ym, y2 = flip_core(t), (t + 2) % N_T, (t + 6) % N_T, (t + 4) % N_T
    h, xp, xm = flip_far(dp), (dp + 4) % N_DP, (dp + 12) % N_DP
    c = flip_core(dp)
    Z, YP, YM = (dp, z), (dp, yp), (dp, ym)
    H, XP, XM, C = (h, t), (xp, t), (xm, t), (c, t)
    x, core = dp // 4, dp % 2
    xpi, xmi, x2i = (x + 1) % 4, (x + 3) % 4, (x + 2) % 4
    zh, zl = (dp // 2) % 2, t % 2
    ypb, ymb, y2b = yp - zl, ym - zl, y2 - zl

    pieces = [(x2i, 0), (x2i, 1), (xpi, 1), (xmi, 0), (xpi, 0), (xmi, 1), (x, 0), (x, 1)]
    order = [(0, 0), (1, 0), (0, 1), (1, 1), (2, 0), (3, 0), (4, 0), (5, 0)]
    order += [(2, 1), (3, 1), (4, 1), (5, 1), (6, 0), (7, 0), (6, 1), (7, 1)]
    place = {item: i for i, item in enumerate(order)}

    def q_load(i):
        k, s = order[i]
        xi, p = pieces[k]
        src = q_ref.at[(xi * 4 + p * 2) + core, pl.ds(s * SR, SR)]
        return pltpu.make_async_copy(src, qv.at[i % QSLOTS], qloc.at[i])

    def w_load(k):
        cols = pl.ds(k * CW, CW)
        return pltpu.make_async_copy(wd_ref.at[:, cols], wd.at[:, cols], wloc.at[k])

    h_load = pltpu.make_async_copy(h_ref, h_v, loc.at[0])
    g_load = pltpu.make_async_copy(g_ref, g_v, loc.at[1])
    for i in range(4):
        q_load(i).start()
    h_load.start()
    for k in range(NCH):
        w_load(k).start()
    for i in range(4, QSLOTS):
        q_load(i).start()
    greet((Z, YP, YM, H, XP, XM, C))

    m, q = Sends(m_send, m_recv), Sends(q_send, q_recv)
    for k, s in order:
        xi, p = pieces[k]
        src = q_ref.at[(xi * 4 + p * 2) + 1 - core, pl.ds(s * SR, SR)]
        q.start(14 + place[k, s], src, qc.at[k, s], C)

    def add_sibling(k, s, extra=()):
        i = place[k, s]
        q.arrived(14 + i, qc.at[k, s], C)
        q_load(i).wait()
        add_rows(qc.at[k, s], [qv.at[i % QSLOTS], qc.at[k, s], *extra], SR, 208)
        if i + QSLOTS < len(order):
            q_load(i + QSLOTS).start()

    def q_relay(s):
        add_sibling(0, s)
        q.start(s, qc.at[0, s], qrel.at[0, s], XP)
        add_sibling(1, s)
        q.start(2 + s, qc.at[1, s], qrel.at[1, s], XM)

    def q_direct(s):
        add_sibling(2, s)
        q.start(4 + s, qc.at[2, s], qm.at[1, s], XP)
        add_sibling(3, s)
        q.start(6 + s, qc.at[3, s], qp.at[0, s], XM)

    def q_forward(s):
        q.arrived(s, qrel.at[0, s], XM)
        add_sibling(4, s, [qrel.at[0, s]])
        q.start(8 + s, qc.at[4, s], qm.at[0, s], XP)
        q.arrived(2 + s, qrel.at[1, s], XP)
        add_sibling(5, s, [qrel.at[1, s]])
        q.start(10 + s, qc.at[5, s], qp.at[1, s], XM)

    def q_far(s):
        add_sibling(6, s)
        add_sibling(7, s)
        q.arrived(4 + s, qm.at[1, s], XM)
        q.arrived(6 + s, qp.at[0, s], XP)
        q.arrived(8 + s, qm.at[0, s], XM)
        q.arrived(10 + s, qp.at[1, s], XP)
        mine = qc.at[7 - zh, s]
        add_rows(mine, [mine, qm.at[1 - zh, s], qp.at[1 - zh, s]], SR, 208)
        q.start(12 + s, mine, qh.at[s], H)

    def q_final(s):
        q.arrived(12 + s, qh.at[s], H)
        total = bg_ref.at[pl.ds(s * SR, SR)]
        add_rows(total, [qc.at[6 + zh, s], qm.at[zh, s], qp.at[zh, s], qh.at[s]], SR, 208)

    def part(k, tt):
        return pv.at[k, pl.ds(pl.multiple_of(tt * TOK, TOK), TOK)]

    def forward(k):
        w_load(k).wait()

        @pl.loop(0, 2)
        def _(i):
            rows = pl.ds(pl.multiple_of(i * (ROWS // 2), ROWS // 2), ROWS // 2)
            pv[k, rows, :] = jnp.dot(
                h_v[rows, :], wd[:, k * CW : (k + 1) * CW], preferred_element_type=F32
            ).astype(BF)

        m.start(7 * k, part(k, y2b), prel.at[0, k], YP)
        m.start(7 * k + 1, part(k, y2b + 1), prel.at[1, k], YM)

    def m_forward(k):
        m.arrived(7 * k, prel.at[0, k], YM)
        add_rows(part(k, ypb), [part(k, ypb), prel.at[0, k]], TOK, 64)
        m.start(7 * k + 4, part(k, ypb), pm.at[0, k], YP)
        m.arrived(7 * k + 1, prel.at[1, k], YP)
        add_rows(part(k, ymb + 1), [part(k, ymb + 1), prel.at[1, k]], TOK, 64)
        m.start(7 * k + 5, part(k, ymb + 1), pp.at[1, k], YM)
        m.start(7 * k + 2, part(k, ypb + 1), pm.at[1, k], YP)
        m.start(7 * k + 3, part(k, ymb), pp.at[0, k], YM)

    def m_near(k):
        m.arrived(7 * k + 4, pm.at[0, k], YM)
        m.arrived(7 * k + 5, pp.at[1, k], YP)
        m.arrived(7 * k + 2, pm.at[1, k], YM)
        m.arrived(7 * k + 3, pp.at[0, k], YP)
        mine = part(k, z)
        add_rows(mine, [mine, pm.at[1 - zl, k], pp.at[1 - zl, k]], TOK, 64)
        m.start(7 * k + 6, mine, pz.at[k], Z)

    def m_final(k):
        m.arrived(7 * k + 6, pz.at[k], Z)
        total = mixed_ref.at[:, pl.ds(k * CW, CW)]
        add_rows(total, [part(k, t), pm.at[zl, k], pp.at[zl, k], pz.at[k]], TOK, 64)

    def b_loads(j):
        cols = pl.ds(j * BN, BN)
        return (
            pltpu.make_async_copy(gate_ref.at[:, cols], gate_v.at[j % 2], bloc.at[0, j]),
            pltpu.make_async_copy(up_ref.at[:, cols], up_v.at[j % 2], bloc.at[1, j]),
        )

    def b_stores(j):
        cols = pl.ds(j * BN, BN)
        return (
            pltpu.make_async_copy(gate_v.at[j % 2], gg_out.at[:, cols], oloc.at[0, j]),
            pltpu.make_async_copy(up_v.at[j % 2], ug_out.at[:, cols], oloc.at[1, j]),
        )

    def backward(j):
        if j == 0:
            g_load.wait()
        if j >= 1:
            for copy in b_stores(j - 1):
                copy.wait()
        if j + 1 < NBW:
            for copy in b_loads(j + 1):
                copy.start()
        for copy in b_loads(j):
            copy.wait()

        @pl.loop(0, 2)
        def _(i):
            rows = pl.ds(pl.multiple_of(i * (ROWS // 2), ROWS // 2), ROWS // 2)
            gh = lax.dot_general(
                g_v[rows, :], wd[j * BN : (j + 1) * BN, :], (((1,), (1,)), ((), ())),
                preferred_element_type=F32,
            )
            gate = gate_v[j % 2, rows, :].astype(F32)
            up = up_v[j % 2, rows, :].astype(F32)
            sig = jax.nn.sigmoid(gate)
            gate_v[j % 2, rows, :] = (gh * up * sig * (1.0 + gate * (1.0 - sig))).astype(BF)
            up_v[j % 2, rows, :] = (gh * gate * sig).astype(BF)

        for copy in b_stores(j):
            copy.start()

    q_relay(0)
    q_relay(1)
    h_load.wait()
    g_load.start()
    for copy in b_loads(0):
        copy.start()
    forward(0)
    q_direct(0)
    forward(1)
    m_forward(0)
    q_forward(0)
    forward(2)
    m_forward(1)
    forward(3)
    m_forward(2)
    q_direct(1)
    forward(4)
    m_forward(3)
    q_forward(1)
    for k in range(5, NCH):
        forward(k)
        m_forward(k - 1)
    m_forward(NCH - 1)
    m_near(0)
    m_near(1)
    m_near(2)
    backward(0)
    backward(1)
    m_near(3)
    q_far(0)
    backward(2)
    backward(3)
    backward(4)
    m_near(4)
    m_final(0)
    m_final(1)
    backward(5)
    m_near(5)
    backward(6)
    q_final(0)
    q_far(1)
    for k in range(2, 6):
        m_final(k)
    m_near(6)
    m_near(7)
    q_final(1)
    m_final(6)
    m_final(7)
    m.finish()
    q.finish()
    for copy in b_stores(NBW - 1):
        copy.wait()


def local(gate_pre, up_pre, out_grad, w_blocks, block_ids):
    scale = 1.0 / math.sqrt(ROWS * N_DP)
    ids = block_ids[0, 0]
    meta = jnp.zeros((META, BLK), BF)
    meta = meta.at[0, :MAXB].set((ids // NDB).astype(BF)).at[1, :MAXB].set((ids % NDB).astype(BF))
    packed = jnp.concatenate([w_blocks.reshape(PIECE, BLK), meta], axis=0)

    sem = pltpu.SemaphoreType.DMA
    g_all, w_all, hid, hid_t = pl.pallas_call(
        gather_kernel,
        out_shape=(
            jax.ShapeDtypeStruct((N_T, TOK, D), BF),
            jax.ShapeDtypeStruct((N_DP, WROWS, BLK), BF),
            jax.ShapeDtypeStruct((ROWS, HID), BF),
            jax.ShapeDtypeStruct((HID, ROWS), BF),
        ),
        in_specs=[ANY] * 4,
        out_specs=[ANY] * 4,
        scratch_shapes=[
            pltpu.VMEM((ROWS, HID), BF),
            pltpu.VMEM((ROWS, HID), BF),
            pltpu.VMEM((ROWS, HID), BF),
            pltpu.VMEM((HID, ROWS), BF),
            sem((11,)), sem((11,)), sem((19,)), sem((19,)), sem((6,)),
        ],
        compiler_params=pltpu.CompilerParams(
            collective_id=0, has_side_effects=True, vmem_limit_bytes=60 * MIB
        ),
        name="gather",
    )(out_grad, packed, gate_pre, up_pre)

    packed_grads, dense = pl.pallas_call(
        functools.partial(weight_kernel, scale),
        out_shape=(
            jax.ShapeDtypeStruct((N_DP, PIECE, BLK), BF),
            jax.ShapeDtypeStruct((HID, D), BF),
        ),
        in_specs=[ANY] * 3,
        out_specs=[ANY] * 2,
        scratch_shapes=[
            pltpu.VMEM((HID, D), BF),
            pltpu.VMEM((HID, ROWS), BF),
            pltpu.VMEM((ROWS, D), BF),
            pltpu.VMEM((NLOC, BLK, BLK), BF),
            pltpu.VMEM((N_DP, META, BLK), BF),
            pltpu.VMEM((N_DP, BLK), jnp.int32),
            pltpu.SMEM((N_DP, BLK), jnp.int32),
            pltpu.VMEM((BLK, BLK), BF),
            sem((5,)), sem, sem,
        ],
        compiler_params=pltpu.CompilerParams(vmem_limit_bytes=60 * MIB),
        name="weight",
    )(hid_t, g_all.reshape(ROWS, D), w_all)

    mixed, grads, gate_grad, up_grad = pl.pallas_call(
        scatter_kernel,
        out_shape=(
            jax.ShapeDtypeStruct((TOK, D), BF),
            jax.ShapeDtypeStruct((PIECE, BLK), F32),
            jax.ShapeDtypeStruct((ROWS, HID), BF),
            jax.ShapeDtypeStruct((ROWS, HID), BF),
        ),
        in_specs=[ANY] * 6,
        out_specs=[VM, VM, ANY, ANY],
        scratch_shapes=[
            pltpu.VMEM((ROWS, HID), BF),
            pltpu.VMEM((HID, D), BF),
            pltpu.VMEM((ROWS, D), BF),
            pltpu.VMEM((2, ROWS, BN), BF),
            pltpu.VMEM((2, ROWS, BN), BF),
            pltpu.VMEM((NCH, ROWS, CW), BF),
            pltpu.VMEM((2, NCH, TOK, CW), BF),
            pltpu.VMEM((2, NCH, TOK, CW), BF),
            pltpu.VMEM((2, NCH, TOK, CW), BF),
            pltpu.VMEM((NCH, TOK, CW), BF),
            pltpu.VMEM((QSLOTS, SR, BLK), BF),
            pltpu.VMEM((8, NSP, SR, BLK), BF),
            pltpu.VMEM((2, NSP, SR, BLK), BF),
            pltpu.VMEM((2, NSP, SR, BLK), BF),
            pltpu.VMEM((2, NSP, SR, BLK), BF),
            pltpu.VMEM((NSP, SR, BLK), BF),
            sem((7 * NCH,)), sem((7 * NCH,)), sem((30,)), sem((30,)),
            sem((2,)), sem((NCH,)), sem((16,)), sem((2, NBW)), sem((2, NBW)),
        ],
        compiler_params=pltpu.CompilerParams(
            collective_id=1, has_side_effects=True, vmem_limit_bytes=63 * MIB
        ),
        name="scatter",
    )(gate_pre, up_pre, hid, dense, g_all.reshape(ROWS, D), packed_grads)
    return mixed, gate_grad, up_grad, grads.reshape(1, 1, MAXB, BLK, BLK)


def solution(mesh):
    placed = (
        P("dp", "tensor"),
        P("dp", "tensor"),
        P(("dp", "tensor"), None),
        P("tensor", "dp", None, None, None),
        P("tensor", "dp", None),
    )
    return jax.shard_map(
        local,
        mesh=mesh,
        in_specs=placed,
        out_specs=(
            P(("dp", "tensor"), None),
            P("dp", "tensor"),
            P("dp", "tensor"),
            P("tensor", "dp", None, None, None),
        ),
        check_vma=False,
    )
```
